32 devices in a mesh: dp: 8 (over z, core), seq: 4 (over y, x).
Axes of the slice: x: 2, y: 2, z: 4, core: 2. Of those that a mesh axis runs over, the one named last changes fastest.
Arguments:
- ssd_input: bfloat16 [8192, 4096], P(('dp', 'seq')), parts along dimension 0, may hold values from -6 to 6
- gate_input: bfloat16 [8192, 4096], P(('dp', 'seq')), parts along dimension 0, may hold values from -6 to 6
- write_map: bfloat16 [8192, 512], P(('dp', 'seq')), parts along dimension 0, may hold values from -6 to 6
- read_map: bfloat16 [8192, 512], P(('dp', 'seq')), parts along dimension 0, may hold values from -6 to 6
- step_size: float32 [8192, 32], P(('dp', 'seq')), parts along dimension 0, may hold values from 0.002 to 12.8, as said below
- decay_log: float32 [32], replicated, as said below
- skip_gain: float32 [32], replicated, may hold values from 0.5 to 1.5
- norm_gain: bfloat16 [4096], replicated, may hold values from 0.099609375 to 1.8984375
- query_rows: bfloat16 [8192, 2048], P(('dp', 'seq')), parts along dimension 0, may hold values from -30 to 30
- key_rows: bfloat16 [8192, 512], P(('dp', 'seq')), parts along dimension 0, may hold values from -4 to 4
- value_rows: bfloat16 [8192, 512], P(('dp', 'seq')), parts along dimension 0, may hold values from -6 to 6
Outputs:
- ssd_out: bfloat16 [8192, 4096], P(('dp', 'seq')), parts along dimension 0
- attn_out: bfloat16 [8192, 2048], P(('dp', 'seq')), parts along dimension 0
The draws below stay inside these ranges and needn't reach their ends.
There are 8 independent parts, one for each index of `dp`. The reference program is written for one: setup_inputs(seed, part) draws one part's arguments, and reference() takes and returns one part's arrays. A program takes and returns all parts, laid end to end along the dimension named above; an argument that names none is the same for every part. Nothing has to cross between parts.
Inputs may be any that keep to these rules, and one draw needn't show every extreme that they name: `step_size`: positive everywhere. Rates exp(decay_log) lie between 30 / 1024 and about 3.4.
All inputs are finite; a program needn't handle non-finite values.
Results may differ from the reference program's by a relative error of at most 0.0059.
Values may be sent and summed in bfloat16 or wider, within the bound.
A program may use at most 192 MiB of HBM per device.

```python
import math
import jax
import jax.numpy as jnp
from jax import lax

TOK_DEV = 256
MANUSCRIPT_SPAN = 1024
SSD_HEADS = 32
HEAD_DIM = 128
STATE = 128
GROUPS = 4
SPAN = 128
Q_HEADS = 16
KV_HEADS = 4
ATT_DIM = 128
N_SEQ = 4


def draw_query_rows(key, part):
    key = jax.random.fold_in(key, 11)
    starting_shift = jnp.clip(jax.random.normal(key, (MANUSCRIPT_SPAN, Q_HEADS, ATT_DIM), jnp.float32), -4.0, 4.0)
    return starting_shift.reshape(MANUSCRIPT_SPAN, Q_HEADS * ATT_DIM).astype(jnp.bfloat16)


def draw_key_rows(key, part):
    key = jax.random.fold_in(key, 12)
    starting_shift = jnp.clip(jax.random.normal(key, (MANUSCRIPT_SPAN, KV_HEADS, ATT_DIM), jnp.float32), -4.0, 4.0)
    return starting_shift.reshape(MANUSCRIPT_SPAN, KV_HEADS * ATT_DIM).astype(jnp.bfloat16)


def draw_step_size(key, part):
    key = jax.random.fold_in(key, 21)
    key_a, key_b, lookup_tertile, key_d, key_e, key_f = jax.random.split(key, 6)
    element_indices = jnp.arange(MANUSCRIPT_SPAN)
    rough = jnp.exp(jax.random.uniform(key_a, (MANUSCRIPT_SPAN, SSD_HEADS), jnp.float32, -math.log(2.0), math.log(2.0)))
    spread = jnp.exp(jax.random.uniform(key_b, (MANUSCRIPT_SPAN // 64 + 1, SSD_HEADS), jnp.float32, -math.log(2.0), math.log(2.0)))
    base_steps = 0.01 * rough * spread[element_indices // 64]
    device_count = MANUSCRIPT_SPAN // TOK_DEV
    volley_device = jax.random.randint(lookup_tertile, (), 0, max(device_count // 4, 1))
    device_of = element_indices // TOK_DEV
    drawn_mask = (device_of > volley_device) & (device_of <= volley_device + device_count // 2)
    drawn_steps = 0.002 * jnp.exp(jax.random.uniform(key_e, (MANUSCRIPT_SPAN, SSD_HEADS), jnp.float32, 0.0, math.log(2.0)))
    step_values = jnp.where(drawn_mask[:, None], drawn_steps, base_steps)
    other_slot = jax.random.randint(key_d, (), 0, MANUSCRIPT_SPAN)
    other_size = 0.01 * MANUSCRIPT_SPAN * jax.random.uniform(key_f, (), jnp.float32, 0.8, 1.15)
    step_values = jnp.where((element_indices == other_slot)[:, None], other_size, step_values)
    edge_slot = (volley_device + 1) * TOK_DEV - 1
    step_values = jnp.where((element_indices == edge_slot)[:, None], 0.0125 * MANUSCRIPT_SPAN, step_values)
    return step_values.astype(jnp.float32)


def draw_decay_log(key, part):
    key = jax.random.fold_in(key, 31)
    key_a, key_b, lookup_tertile = jax.random.split(key, 3)
    fast_count = SSD_HEADS // 2
    head_order = jax.random.permutation(key_a, SSD_HEADS)
    fast = head_order < fast_count
    fast_rate = jnp.exp(jax.random.uniform(key_b, (SSD_HEADS,), jnp.float32, math.log(1.0 / 60.0), math.log(1.0 / 30.0))) / 0.01
    slow_rate = jnp.exp(jax.random.uniform(lookup_tertile, (SSD_HEADS,), jnp.float32, math.log(0.3), math.log(0.6))) / (0.01 * MANUSCRIPT_SPAN)
    return jnp.log(jnp.where(fast, fast_rate, slow_rate)).astype(jnp.float32)


def level_of(stream_key, shape, cuts, low, high):
    gain = 1.0
    for axis_at, blocks in cuts:
        heights = jax.random.uniform(jax.random.fold_in(jax.random.fold_in(stream_key, 6), axis_at), (blocks,), jnp.float32, low / len(cuts), high / len(cuts))
        gain = gain * jnp.repeat(jnp.exp(heights), shape[axis_at] // blocks).reshape((-1,) + (1,) * (len(shape) - 1 - axis_at))
    return gain


def normal_values(rng, dims, scale, most, shards=(), kind=jnp.bfloat16):
    values = scale * jax.random.normal(rng, dims, jnp.float32)
    if shards:
        values = values * level_of(rng, dims, shards, -0.22, 0.18)
    return jnp.clip(values, -most, most).astype(kind)


def setup_inputs(seed: int = 0, part: int = 0) -> dict:
    key_list = jax.random.split(jax.random.key(seed), 12)
    own_keys = jax.random.split(jax.random.fold_in(key_list[11], part), 12)
    ssd_input = normal_values(own_keys[0], (MANUSCRIPT_SPAN, SSD_HEADS * HEAD_DIM), 1.0, 6.0, ((0, 4),))
    gate_input = normal_values(own_keys[1], (MANUSCRIPT_SPAN, SSD_HEADS * HEAD_DIM), 1.0, 6.0, ((0, 4),))
    write_map = normal_values(own_keys[2], (MANUSCRIPT_SPAN, GROUPS * STATE), 1.0, 6.0, ((0, 4),))
    read_map = normal_values(own_keys[3], (MANUSCRIPT_SPAN, GROUPS * STATE), 1.0, 6.0, ((0, 4),))
    step_size = draw_step_size(jax.random.fold_in(jax.random.fold_in(key_list[11], part), 71), part)
    decay_log = draw_decay_log(jax.random.fold_in(key_list[11], 71), part)
    skip_gain = jnp.clip(jax.random.uniform(key_list[6], (SSD_HEADS,), jnp.float32, 0.5, 1.5), 0.5, 1.5)
    norm_gain = jnp.clip(1.0 + 0.18 * jax.random.normal(key_list[7], (SSD_HEADS * HEAD_DIM,), jnp.float32), 0.099609375, 1.8984375).astype(jnp.bfloat16)
    query_rows = draw_query_rows(jax.random.fold_in(jax.random.fold_in(key_list[11], part), 71), part)
    key_rows = draw_key_rows(jax.random.fold_in(jax.random.fold_in(key_list[11], part), 71), part)
    value_rows = normal_values(own_keys[10], (MANUSCRIPT_SPAN, KV_HEADS * ATT_DIM), 1.0, 6.0, ((0, 4),))
    return {"ssd_input": ssd_input, "gate_input": gate_input, "write_map": write_map, "read_map": read_map, "step_size": step_size, "decay_log": decay_log, "skip_gain": skip_gain, "norm_gain": norm_gain, "query_rows": query_rows, "key_rows": key_rows, "value_rows": value_rows}


def gated_norm(mixed_out, gate_input, norm_gain):
    row_count = mixed_out.shape[0]
    gated_y = mixed_out * jax.nn.silu(gate_input.astype(jnp.float32))
    grouped = gated_y.reshape(row_count, GROUPS, -1)
    inverse = lax.rsqrt(lax.optimization_barrier(jnp.mean(grouped * grouped, axis=-1, keepdims=True)) + 1e-05)
    normed = (grouped * inverse).reshape(row_count, -1)
    return (normed * norm_gain.astype(jnp.float32)).astype(jnp.bfloat16)

def round_trip(values):
    return lax.optimization_barrier(values.astype(jnp.bfloat16)).astype(jnp.float32)

def ssd_reference(ssd_input, write_map, read_map, step_size, decay_log, skip_gain):
    per_group = SSD_HEADS // GROUPS
    n_spans = MANUSCRIPT_SPAN // SPAN
    decay_rate = (-jnp.exp(decay_log)).reshape(GROUPS, per_group)
    skip_heads = skip_gain.reshape(GROUPS, per_group)
    inputs_x = ssd_input.reshape(n_spans, SPAN, GROUPS, per_group, HEAD_DIM).astype(jnp.float32)
    write_vals = write_map.reshape(n_spans, SPAN, GROUPS, STATE).astype(jnp.float32)
    read_vals = read_map.reshape(n_spans, SPAN, GROUPS, STATE).astype(jnp.float32)
    steps_dt = step_size.reshape(n_spans, SPAN, GROUPS, per_group)
    causal = jnp.tril(jnp.ones((SPAN, SPAN), dtype=bool))
    highest = lax.Precision.HIGHEST

    def one_span(carry_state, pieces):
        span_x, span_w, span_r, span_dt = pieces
        cumulative = jnp.cumsum(span_dt * decay_rate, axis=0)
        log_gap = cumulative[:, None] - cumulative[None, :]
        decay_mat = jnp.where(causal[:, :, None, None], jnp.exp(jnp.minimum(log_gap, 0.0)), 0.0)
        intersection = jnp.einsum('tgn,sgn->tsg', span_r, span_w, precision=highest)
        weights = round_trip(intersection[..., None] * decay_mat * span_dt[None])
        local_y = jnp.einsum('tsgj,sgjp->tgjp', weights, span_x, precision=highest)
        state_read = round_trip(carry_state)
        carried = jnp.einsum('tgn,gjnp->tgjp', span_r, state_read, precision=highest) * jnp.exp(cumulative)[..., None]
        to_end = jnp.exp(cumulative[-1][None] - cumulative) * span_dt
        scaled = round_trip(to_end[..., None] * span_x)
        fresh = jnp.einsum('sgn,sgjp->gjnp', span_w, scaled, precision=highest)
        new_state = jnp.exp(cumulative[-1])[..., None, None] * carry_state + fresh
        return (new_state, local_y + carried + skip_heads[:, :, None] * span_x)
    zero_state = jnp.zeros((GROUPS, per_group, STATE, HEAD_DIM), jnp.float32)
    final_state, outputs = lax.scan(one_span, zero_state, (inputs_x, write_vals, read_vals, steps_dt))
    return outputs.reshape(MANUSCRIPT_SPAN, SSD_HEADS * HEAD_DIM)

def attention_reference(query_rows, key_rows, value_rows):
    group_size = Q_HEADS // KV_HEADS
    queries = query_rows.reshape(MANUSCRIPT_SPAN, KV_HEADS, group_size, ATT_DIM).astype(jnp.float32)
    key_all = key_rows.reshape(MANUSCRIPT_SPAN, KV_HEADS, ATT_DIM).astype(jnp.float32)
    value_all = value_rows.reshape(MANUSCRIPT_SPAN, KV_HEADS, ATT_DIM).astype(jnp.float32)
    key_pos = jnp.arange(MANUSCRIPT_SPAN, dtype=jnp.int32)
    score_scale = ATT_DIM ** (-0.5)

    def one_block(start_row):
        block_q = lax.dynamic_slice_in_dim(queries, start_row, TOK_DEV, 0)
        q_pos = start_row + jnp.arange(TOK_DEV, dtype=jnp.int32)
        scores = jnp.einsum('rhgd,khd->hgrk', block_q, key_all) * score_scale
        visible = key_pos[None, :] <= q_pos[:, None]
        scores = jnp.where(visible, scores, -1e+30)
        row_max = lax.optimization_barrier(jnp.max(scores, axis=-1, keepdims=True))
        exps = jnp.where(visible, jnp.exp(scores - row_max), 0.0)
        weight_sum = lax.optimization_barrier(jnp.sum(exps, axis=-1))
        softmax_w = lax.optimization_barrier(exps.astype(jnp.bfloat16)).astype(jnp.float32)
        context = jnp.einsum('hgrk,khd->rhgd', softmax_w, value_all)
        context = context / jnp.transpose(weight_sum, (2, 0, 1))[..., None]
        return context.reshape(TOK_DEV, -1).astype(jnp.bfloat16)
    starts = jnp.arange(N_SEQ, dtype=jnp.int32) * TOK_DEV
    return lax.map(one_block, starts).reshape(MANUSCRIPT_SPAN, Q_HEADS * ATT_DIM)

def reference(ssd_input, gate_input, write_map, read_map, step_size, decay_log, skip_gain, norm_gain, query_rows, key_rows, value_rows):
    mixed_out = ssd_reference(ssd_input, write_map, read_map, step_size, decay_log, skip_gain)
    ssd_out = gated_norm(mixed_out, gate_input, norm_gain)
    attn_out = attention_reference(query_rows, key_rows, value_rows)
    return (ssd_out, attn_out)
```

```python
import functools
import math

import jax
import jax.numpy as jnp
from jax import lax
from jax.experimental import pallas as pl
from jax.experimental.pallas import tpu as pltpu
from jax.sharding import PartitionSpec as P

HEAD_DIM = 128
STATE = 128
GROUPS = 4
PER_GROUP = 8
SPAN = 128
Q_HEADS = 16
KV_HEADS = 4
REP = Q_HEADS // KV_HEADS
ATT_DIM = 128
WIDE = PER_GROUP * HEAD_DIM
F32 = jnp.float32
BF16 = jnp.bfloat16
LOWEST = 125.0 * math.log(2.0)
REACH = 250.0 * math.log(2.0)
NT = (((1,), (1,)), ((), ()))
TN = (((0,), (0,)), ((), ()))


def lanes(start, size):
    return pl.ds(pl.multiple_of(start, 128), size)


def coded(value, most):
    root = jnp.sqrt(jnp.abs(value) * (1.0 / most))
    size = jnp.exp(root * REACH - LOWEST)
    return jnp.where(value < 0.0, -size, size).astype(BF16)


def decoded(code, most):
    wide = code.astype(F32)
    root = jnp.maximum(jnp.log(jnp.abs(wide)) + LOWEST, 0.0) * (1.0 / REACH)
    size = root * root * most
    return jnp.where(wide < 0.0, -size, size)


def largest(value):
    column = jnp.max(jnp.abs(value), axis=0, keepdims=True)
    most = jnp.max(column, axis=1, keepdims=True)
    return jnp.broadcast_to(jnp.maximum(most, 1e-30), (1, 128))


def remote(src, dst, send, recv, target):
    return pltpu.make_async_remote_copy(
        src_ref=src,
        dst_ref=dst,
        send_sem=send,
        recv_sem=recv,
        device_id={"seq": target},
        device_id_type=pl.DeviceIdType.MESH,
    )


def kernel(
    n,
    n1,
    n2,
    x_ref,
    gate_ref,
    w_ref,
    r_ref,
    step_ref,
    dlog_ref,
    skip_ref,
    gain_ref,
    q_ref,
    k_ref,
    v_ref,
    ssd_ref,
    att_ref,
    kbuf,
    vbuf,
    row_s,
    col_s,
    row_d,
    col_d,
    row_m,
    col_m,
    fin,
    cum_g,
    te_g,
    ec_g,
    cum_t,
    dt_t,
    st0,
    inc,
    loc,
    acc,
    mx,
    ls,
    kv_send,
    kv_recv,
    row_send,
    row_recv,
    col_send,
    col_recv,
    rm_send,
    rm_recv,
    cm_send,
    cm_recv,
    rd_send,
    rd_recv,
    cd_send,
    cd_recv,
):
    me = lax.axis_index("seq")
    a = me // n2
    b = me % n2
    rows = x_ref.shape[0]
    spans = rows // SPAN
    scale = ATT_DIM**-0.5

    barrier = pltpu.get_barrier_semaphore()

    def greet(i, _):
        pl.semaphore_signal(
            barrier,
            inc=1,
            device_id={"seq": lax.rem(me + i, n)},
            device_id_type=pl.DeviceIdType.MESH,
        )
        return _

    lax.fori_loop(1, n, greet, 0)
    pl.semaphore_wait(barrier, n - 1)

    def k_copy(src, dst):
        return remote(k_ref, kbuf.at[src], kv_send.at[0, dst], kv_recv.at[0, src], dst)

    def v_copy(src, dst):
        return remote(v_ref, vbuf.at[src], kv_send.at[1, dst], kv_recv.at[1, src], dst)

    def send_kv(d, _):
        k_copy(me, d).start()
        v_copy(me, d).start()
        return _

    lax.fori_loop(me + 1, n, send_kv, 0)

    def row_needed(i):
        return (i != b) & ((i > b) | (a < n1 - 1))

    def row_comes(i):
        return (i != b) & ((i < b) | (a < n1 - 1))

    def row_copy(src, dst, g):
        return remote(
            row_s.at[src, g], row_s.at[src, g], row_send.at[dst, g], row_recv.at[src, g], a * n2 + dst
        )

    def rm_copy(src, dst, g):
        return remote(
            row_m.at[src, g], row_m.at[src, g], rm_send.at[dst, g], rm_recv.at[src, g], a * n2 + dst
        )

    def rd_copy(src, dst):
        return remote(row_d.at[src], row_d.at[src], rd_send.at[dst], rd_recv.at[src], a * n2 + dst)

    def col_copy(src, dst, g):
        return remote(
            col_s.at[src, g], col_s.at[src, g], col_send.at[dst, g], col_recv.at[src, g], dst * n2 + b
        )

    def cm_copy(src, dst, g):
        return remote(
            col_m.at[src, g], col_m.at[src, g], cm_send.at[dst, g], cm_recv.at[src, g], dst * n2 + b
        )

    def cd_copy(src, dst):
        return remote(col_d.at[src], col_d.at[src], cd_send.at[dst], cd_recv.at[src], dst * n2 + b)

    def each(lo, hi, needed, act):
        def body(i, _):
            @pl.when(needed(i))
            def _go():
                act(i)

            return _

        lax.fori_loop(lo, hi, body, 0)

    rate = -jnp.exp(dlog_ref[...])
    below = lax.broadcasted_iota(jnp.int32, (SPAN, SPAN), 0)
    along = lax.broadcasted_iota(jnp.int32, (SPAN, SPAN), 1)
    causal = below >= along
    tri = causal.astype(F32)
    total = jnp.zeros((GROUPS * PER_GROUP, 1), F32)
    for c in range(spans):
        at = slice(c * SPAN, (c + 1) * SPAN)
        dt = step_ref[at, :]
        cum = jnp.dot(tri, dt * rate, precision=lax.Precision.HIGHEST, preferred_element_type=F32)
        cum_tr = cum.T
        te = jnp.exp(cum[SPAN - 1 :, :] - cum) * dt
        ec = jnp.exp(cum)
        for g in range(GROUPS):
            hs = slice(g * PER_GROUP, (g + 1) * PER_GROUP)
            cum_g[g, at, :] = cum[:, hs]
            te_g[g, at, :] = te[:, hs]
            ec_g[g, at, :] = ec[:, hs]
        cum_t[:, at] = cum_tr
        dt_t[:, at] = dt.T
        total = total + cum_tr[:, SPAN - 1 :]
    for g in range(GROUPS):
        hs = slice(g * PER_GROUP, (g + 1) * PER_GROUP)
        row_d[b, g, :, :] = jnp.broadcast_to(jnp.exp(total[hs, :]), (PER_GROUP, 128))
    each(0, n2, row_needed, lambda i: rd_copy(b, i).start())

    def end_decay(c, g):
        ends = cum_t[pl.ds(pl.multiple_of(g * PER_GROUP, 8), PER_GROUP), c * SPAN : (c + 1) * SPAN]
        return jnp.exp(jnp.broadcast_to(ends[:, SPAN - 1 :], (PER_GROUP, 128)))

    def states(g, _):
        for c in range(spans):
            at = slice(c * SPAN, (c + 1) * SPAN)
            te = te_g[g, at, :]
            wv = w_ref[at, lanes(g * STATE, STATE)]
            ed = end_decay(c, g)
            scaled = []
            for j in range(PER_GROUP):
                xv = x_ref[at, lanes(g * WIDE + j * HEAD_DIM, HEAD_DIM)].astype(F32)
                scaled.append((te[:, j : j + 1] * xv).astype(BF16))
            for j in range(0, PER_GROUP, 2):
                fresh = lax.dot_general(
                    wv, jnp.concatenate(scaled[j : j + 2], axis=1), TN, preferred_element_type=F32
                )
                for o in range(2):
                    js = slice((j + o) * HEAD_DIM, (j + o + 1) * HEAD_DIM)
                    part = fresh[:, o * HEAD_DIM : (o + 1) * HEAD_DIM]
                    if c:
                        part = ed[j + o : j + o + 1, :] * st0[c - 1, g, :, js] + part
                    if c < spans - 1:
                        st0[c, g, :, js] = part
                    else:
                        fin[g, :, js] = part
                        most = largest(part)
                        row_m[b, g, j + o : j + o + 1, :] = most
                        row_s[b, g, :, js] = coded(part, most)

        def go(i):
            rm_copy(b, i, g).start()
            row_copy(b, i, g).start()

        each(0, n2, row_needed, go)
        return _

    lax.fori_loop(0, GROUPS, states, 0)

    def within(g, _):
        for c in range(spans):
            at = slice(c * SPAN, (c + 1) * SPAN)
            rv = r_ref[at, lanes(g * STATE, STATE)]
            wv = w_ref[at, lanes(g * STATE, STATE)]
            cross = lax.dot_general(rv, wv, NT, preferred_element_type=F32)
            hs = pl.ds(pl.multiple_of(g * PER_GROUP, 8), PER_GROUP)
            cum_rows = cum_t[hs, at]
            dt_rows = dt_t[hs, at]
            cum_cols = cum_g[g, at, :]
            for j in range(PER_GROUP):
                gap = cum_cols[:, j : j + 1] - cum_rows[j : j + 1, :]
                decay = jnp.exp(jnp.where(causal, jnp.minimum(gap, 0.0), -1e30))
                weights = (cross * decay * dt_rows[j : j + 1, :]).astype(BF16)
                xv = x_ref[at, lanes(g * WIDE + j * HEAD_DIM, HEAD_DIM)]
                y = jnp.dot(weights, xv, preferred_element_type=F32)
                loc[at, lanes(g * WIDE + j * HEAD_DIM, HEAD_DIM)] = (
                    y + skip_ref[g * PER_GROUP + j] * xv.astype(F32)
                )
        return _

    lax.fori_loop(0, GROUPS, within, 0)

    seen = lax.broadcasted_iota(jnp.int32, (rows, rows), 0) >= lax.broadcasted_iota(
        jnp.int32, (rows, rows), 1
    )

    def own(h, _):
        kv = k_ref[:, lanes(h * ATT_DIM, ATT_DIM)]
        vv = v_ref[:, lanes(h * ATT_DIM, ATT_DIM)]
        for r in range(REP):
            at = lanes((h * REP + r) * ATT_DIM, ATT_DIM)
            s = lax.dot_general(q_ref[:, at], kv, NT, preferred_element_type=F32) * scale
            s = jnp.where(seen, s, -1e30)
            top = jnp.max(s, axis=-1, keepdims=True)
            p = jnp.exp(s - top)
            mx[h * REP + r] = jnp.broadcast_to(top, (rows, 128))
            ls[h * REP + r] = jnp.broadcast_to(jnp.sum(p, axis=-1, keepdims=True), (rows, 128))
            acc[:, at] = jnp.dot(p.astype(BF16), vv, preferred_element_type=F32)
        return _

    lax.fori_loop(0, KV_HEADS, own, 0)

    each(0, n2, row_comes, lambda i: rd_copy(i, b).wait_recv())

    @pl.when(a < n1 - 1)
    def _row_total():
        col_d[a] = lax.fori_loop(
            0, n2, lambda i, d: d * row_d[i], jnp.ones((GROUPS, PER_GROUP, 128), F32)
        )

    each(0, n1, lambda i: i > a, lambda i: cd_copy(a, i).start())

    def row_phase(g, _):
        def come(i):
            rm_copy(i, b, g).wait_recv()
            row_copy(i, b, g).wait_recv()

        each(0, n2, row_comes, come)
        for j in range(PER_GROUP):
            js = slice(j * HEAD_DIM, (j + 1) * HEAD_DIM)

            def fold(i, t, j=j, js=js):
                new = decoded(row_s[i, g, :, js], row_m[i, g, j : j + 1, :])
                return row_d[i, g, j : j + 1, :] * t + new

            before = lax.fori_loop(0, b, fold, jnp.zeros((STATE, HEAD_DIM), F32))
            inc[g, :, js] = before

            @pl.when(a < n1 - 1)
            def _all(before=before, fold=fold, j=j, js=js):
                mine = row_d[b, g, j : j + 1, :] * before + fin[g, :, js]
                whole = lax.fori_loop(b + 1, n2, fold, mine)
                most = largest(whole)
                col_m[a, g, j : j + 1, :] = most
                col_s[a, g, :, js] = coded(whole, most)

        def go(i):
            cm_copy(a, i, g).start()
            col_copy(a, i, g).start()

        each(0, n1, lambda i: i > a, go)
        return _

    lax.fori_loop(0, GROUPS, row_phase, 0)

    def earlier(src, _):
        k_copy(src, me).wait_recv()
        v_copy(src, me).wait_recv()

        def heads(h, _):
            kv = kbuf[src, :, lanes(h * ATT_DIM, ATT_DIM)]
            vv = vbuf[src, :, lanes(h * ATT_DIM, ATT_DIM)]
            for r in range(REP):
                at = lanes((h * REP + r) * ATT_DIM, ATT_DIM)
                s = lax.dot_general(q_ref[:, at], kv, NT, preferred_element_type=F32) * scale
                old = mx[h * REP + r]
                top = jnp.maximum(old, jnp.max(s, axis=-1, keepdims=True))
                factor = jnp.exp(old - top)
                p = jnp.exp(s - jnp.concatenate([top] * (rows // 128), axis=1))
                mx[h * REP + r] = top
                ls[h * REP + r] = ls[h * REP + r] * factor + jnp.sum(p, axis=-1, keepdims=True)
                acc[:, at] = acc[:, at] * factor + jnp.dot(
                    p.astype(BF16), vv, preferred_element_type=F32
                )
            return _

        lax.fori_loop(0, KV_HEADS, heads, 0)
        return _

    lax.fori_loop(0, me, earlier, 0)

    def close(h, _):
        at = lanes(h * ATT_DIM, ATT_DIM)
        att_ref[:, at] = (acc[:, at] / ls[h]).astype(BF16)
        return _

    lax.fori_loop(0, Q_HEADS, close, 0)

    each(0, n1, lambda i: i < a, lambda i: cd_copy(i, a).wait_recv())

    def finish(g, _):
        def come(i):
            cm_copy(i, a, g).wait_recv()
            col_copy(i, a, g).wait_recv()

        each(0, n1, lambda i: i < a, come)
        pre = lax.fori_loop(0, b, lambda i, d: d * row_d[i, g], jnp.ones((PER_GROUP, 128), F32))
        for j in range(PER_GROUP):
            js = slice(j * HEAD_DIM, (j + 1) * HEAD_DIM)

            def fold(i, t, j=j, js=js):
                new = decoded(col_s[i, g, :, js], col_m[i, g, j : j + 1, :])
                return col_d[i, g, j : j + 1, :] * t + new

            above = lax.fori_loop(0, a, fold, jnp.zeros((STATE, HEAD_DIM), F32))
            inc[g, :, js] = inc[g, :, js] + pre[j : j + 1, :] * above
        before = jnp.ones((PER_GROUP, 128), F32)
        for c in range(spans):
            at = slice(c * SPAN, (c + 1) * SPAN)
            rv = r_ref[at, lanes(g * STATE, STATE)]
            ec = ec_g[g, at, :]
            square = jnp.zeros((SPAN, HEAD_DIM), F32)
            for j in range(0, PER_GROUP, 2):
                starts = []
                for o in range(2):
                    js = slice((j + o) * HEAD_DIM, (j + o + 1) * HEAD_DIM)
                    start = inc[g, :, js]
                    if c:
                        start = before[j + o : j + o + 1, :] * start + st0[c - 1, g, :, js]
                    starts.append(start.astype(BF16))
                read = jnp.dot(rv, jnp.concatenate(starts, axis=1), preferred_element_type=F32)
                for o in range(2):
                    hs = lanes(g * WIDE + (j + o) * HEAD_DIM, HEAD_DIM)
                    mixed = (
                        loc[at, hs]
                        + read[:, o * HEAD_DIM : (o + 1) * HEAD_DIM] * ec[:, j + o : j + o + 1]
                    )
                    v = gate_ref[at, hs].astype(F32)
                    gated = mixed * (v / (1.0 + jnp.exp(-v)))
                    loc[at, hs] = gated
                    square = square + gated * gated
            mean = jnp.sum(square, axis=-1, keepdims=True) / WIDE
            inverse = lax.rsqrt(mean + 1e-05)
            for j in range(PER_GROUP):
                hs = lanes(g * WIDE + j * HEAD_DIM, HEAD_DIM)
                ssd_ref[at, hs] = (loc[at, hs] * inverse * gain_ref[:, hs].astype(F32)).astype(BF16)
            before = before * end_decay(c, g)
        return _

    lax.fori_loop(0, GROUPS, finish, 0)

    def sent_kv(d, _):
        k_copy(me, d).wait_send()
        v_copy(me, d).wait_send()
        return _

    lax.fori_loop(me + 1, n, sent_kv, 0)
    each(0, n2, row_needed, lambda i: rd_copy(b, i).wait_send())
    each(0, n1, lambda i: i > a, lambda i: cd_copy(a, i).wait_send())

    def sent(g, _):
        def row_left(i):
            rm_copy(b, i, g).wait_send()
            row_copy(b, i, g).wait_send()

        def col_left(i):
            cm_copy(a, i, g).wait_send()
            col_copy(a, i, g).wait_send()

        each(0, n2, row_needed, row_left)
        each(0, n1, lambda i: i > a, col_left)
        return _

    lax.fori_loop(0, GROUPS, sent, 0)


def local(
    n,
    ssd_input,
    gate_input,
    write_map,
    read_map,
    step_size,
    decay_log,
    skip_gain,
    norm_gain,
    query_rows,
    key_rows,
    value_rows,
):
    n2 = math.isqrt(n)
    while n % n2:
        n2 -= 1
    n1 = n // n2
    rows = ssd_input.shape[0]
    spans = rows // SPAN
    heads = GROUPS * PER_GROUP
    vmem = pl.BlockSpec(memory_space=pltpu.VMEM)
    smem = pl.BlockSpec(memory_space=pltpu.SMEM)
    dma = pltpu.SemaphoreType.DMA
    return pl.pallas_call(
        functools.partial(kernel, n, n1, n2),
        out_shape=(
            jax.ShapeDtypeStruct(ssd_input.shape, BF16),
            jax.ShapeDtypeStruct(query_rows.shape, BF16),
        ),
        in_specs=[vmem, vmem, vmem, vmem, vmem, vmem, smem, vmem, vmem, vmem, vmem],
        out_specs=(vmem, vmem),
        scratch_shapes=[
            pltpu.VMEM((n,) + key_rows.shape, BF16),
            pltpu.VMEM((n,) + value_rows.shape, BF16),
            pltpu.VMEM((n2, GROUPS, STATE, WIDE), BF16),
            pltpu.VMEM((n1, GROUPS, STATE, WIDE), BF16),
            pltpu.VMEM((n2, GROUPS, PER_GROUP, 128), F32),
            pltpu.VMEM((n1, GROUPS, PER_GROUP, 128), F32),
            pltpu.VMEM((n2, GROUPS, PER_GROUP, 128), F32),
            pltpu.VMEM((n1, GROUPS, PER_GROUP, 128), F32),
            pltpu.VMEM((GROUPS, STATE, WIDE), F32),
            pltpu.VMEM((GROUPS, rows, PER_GROUP), F32),
            pltpu.VMEM((GROUPS, rows, PER_GROUP), F32),
            pltpu.VMEM((GROUPS, rows, PER_GROUP), F32),
            pltpu.VMEM((heads, rows), F32),
            pltpu.VMEM((heads, rows), F32),
            pltpu.VMEM((spans - 1, GROUPS, STATE, WIDE), F32),
            pltpu.VMEM((GROUPS, STATE, WIDE), F32),
            pltpu.VMEM(ssd_input.shape, F32),
            pltpu.VMEM(query_rows.shape, F32),
            pltpu.VMEM((Q_HEADS, rows, 128), F32),
            pltpu.VMEM((Q_HEADS, rows, 128), F32),
            dma((2, n)),
            dma((2, n)),
            dma((n2, GROUPS)),
            dma((n2, GROUPS)),
            dma((n1, GROUPS)),
            dma((n1, GROUPS)),
            dma((n2, GROUPS)),
            dma((n2, GROUPS)),
            dma((n1, GROUPS)),
            dma((n1, GROUPS)),
            dma((n2,)),
            dma((n2,)),
            dma((n1,)),
            dma((n1,)),
        ],
        compiler_params=pltpu.CompilerParams(
            collective_id=0, has_side_effects=True, vmem_limit_bytes=58 * 2**20
        ),
        cost_estimate=pl.CostEstimate(
            flops=4 * 10**9, bytes_accessed=12 * 2**20, transcendentals=6 * 10**6
        ),
        name="hybrid_cores",
    )(
        ssd_input,
        gate_input,
        write_map,
        read_map,
        step_size,
        decay_log.reshape(1, -1),
        skip_gain,
        norm_gain.reshape(1, -1),
        query_rows,
        key_rows,
        value_rows,
    )


def solution(mesh):
    split = P(("dp", "seq"), None)
    in_specs = (split, split, split, split, split, P(), P(), P(), split, split, split)
    body = functools.partial(local, mesh.shape["seq"])
    return jax.shard_map(
        body, mesh=mesh, in_specs=in_specs, out_specs=(split, split), check_vma=False
    )
```

```python
import functools
import math

import jax
import jax.numpy as jnp
from jax import lax
from jax.experimental import pallas as pl
from jax.experimental.pallas import tpu as pltpu
from jax.sharding import PartitionSpec as P

HEAD_DIM = 128
STATE = 128
GROUPS = 4
PER_GROUP = 8
SPAN = 128
Q_HEADS = 16
KV_HEADS = 4
REP = Q_HEADS // KV_HEADS
ATT_DIM = 128
WIDE = PER_GROUP * HEAD_DIM
F32 = jnp.float32
BF16 = jnp.bfloat16
LOWEST = 125.0 * math.log(2.0)
REACH = 250.0 * math.log(2.0)
NT = (((1,), (1,)), ((), ()))
TN = (((0,), (0,)), ((), ()))


def lanes(start, size):
    return pl.ds(pl.multiple_of(start, 128), size)


def coded(value, most):
    root = jnp.sqrt(jnp.abs(value) * (1.0 / most))
    size = jnp.exp(root * REACH - LOWEST)
    return jnp.where(value < 0.0, -size, size).astype(BF16)


def decoded(code, most):
    wide = code.astype(F32)
    root = jnp.maximum(jnp.log(jnp.abs(wide)) + LOWEST, 0.0) * (1.0 / REACH)
    size = root * root * most
    return jnp.where(wide < 0.0, -size, size)


def largest(value):
    column = jnp.max(jnp.abs(value), axis=0, keepdims=True)
    most = jnp.max(column, axis=1, keepdims=True)
    return jnp.broadcast_to(jnp.maximum(most, 1e-30), (1, 128))


def remote(src, dst, send, recv, target):
    return pltpu.make_async_remote_copy(
        src_ref=src,
        dst_ref=dst,
        send_sem=send,
        recv_sem=recv,
        device_id={"seq": target},
        device_id_type=pl.DeviceIdType.MESH,
    )


def kernel(
    n,
    n1,
    n2,
    x_hbm,
    gate_hbm,
    w_ref,
    r_hbm,
    step_ref,
    dlog_ref,
    skip_ref,
    gain_ref,
    q_hbm,
    k_ref,
    v_ref,
    ssd_ref,
    att_ref,
    kbuf,
    vbuf,
    row_s,
    col_s,
    row_d,
    col_d,
    row_m,
    col_m,
    fin,
    gains,
    x_ref,
    gate_ref,
    r_ref,
    q_ref,
    load,
    cum_g,
    te_g,
    ec_g,
    cum_t,
    dt_t,
    st0,
    inc,
    loc,
    acc,
    mx,
    ls,
    key_row,
    key_col,
    val_row,
    val_col,
    kv_recv,
    row_send,
    row_recv,
    col_send,
    col_recv,
    rm_send,
    rm_recv,
    cm_send,
    cm_recv,
    rd_send,
    rd_recv,
    cd_send,
    cd_recv,
):
    me = lax.axis_index("seq")
    a = me // n2
    b = me % n2
    rows = x_hbm.shape[0]
    spans = rows // SPAN
    scale = ATT_DIM**-0.5

    loads = [
        pltpu.make_async_copy(src, dst, load.at[i])
        for i, (src, dst) in enumerate(
            ((x_hbm, x_ref), (r_hbm, r_ref), (q_hbm, q_ref), (gate_hbm, gate_ref))
        )
    ]
    loads[0].start()

    barrier = pltpu.get_barrier_semaphore()

    def greet(i, _):
        pl.semaphore_signal(
            barrier,
            inc=1,
            device_id={"seq": lax.rem(me + i, n)},
            device_id_type=pl.DeviceIdType.MESH,
        )
        return _

    lax.fori_loop(1, n, greet, 0)
    pl.semaphore_wait(barrier, n - 1)

    def each(lo, hi, needed, act):
        def body(i, _):
            @pl.when(needed(i))
            def _go():
                act(i)

            return _

        lax.fori_loop(lo, hi, body, 0)

    def key_copy(src_a, dst_b):
        src = src_a * n2 + b
        return remote(
            kbuf.at[src], kbuf.at[src], key_row.at[src_a, dst_b], kv_recv.at[0, src], a * n2 + dst_b
        )

    def key_down(dst_a):
        return remote(k_ref, kbuf.at[me], key_col.at[dst_a], kv_recv.at[0, me], dst_a * n2 + b)

    def key_own(dst_b):
        return remote(k_ref, kbuf.at[me], key_row.at[a, dst_b], kv_recv.at[0, me], a * n2 + dst_b)

    def value_copy(src_b, dst_a):
        src = a * n2 + src_b
        return remote(
            vbuf.at[src], vbuf.at[src], val_col.at[src_b, dst_a], kv_recv.at[1, src], dst_a * n2 + b
        )

    def value_down(dst_a):
        return remote(v_ref, vbuf.at[me], val_col.at[b, dst_a], kv_recv.at[1, me], dst_a * n2 + b)

    def value_own(dst_b):
        return remote(v_ref, vbuf.at[me], val_row.at[dst_b], kv_recv.at[1, me], a * n2 + dst_b)

    def got(which, src):
        return remote(k_ref, kbuf.at[src], key_col.at[0], kv_recv.at[which, src], src).wait_recv()

    def below_me(i):
        return i > a

    def row_needed(i):
        return (i != b) & ((i > b) | (a < n1 - 1))

    def row_comes(i):
        return (i != b) & ((i < b) | (a < n1 - 1))

    each(0, n1, below_me, lambda i: key_down(i).start())
    each(0, n2, row_needed, lambda i: value_own(i).start())
    each(0, n1, below_me, lambda i: value_down(i).start())
    for later in loads[1:]:
        later.start()

    def row_copy(src, dst, g):
        return remote(
            row_s.at[src, g], row_s.at[src, g], row_send.at[dst, g], row_recv.at[src, g], a * n2 + dst
        )

    def rm_copy(src, dst, g):
        return remote(
            row_m.at[src, g], row_m.at[src, g], rm_send.at[dst, g], rm_recv.at[src, g], a * n2 + dst
        )

    def rd_copy(src, dst):
        return remote(row_d.at[src], row_d.at[src], rd_send.at[dst], rd_recv.at[src], a * n2 + dst)

    def col_copy(src, dst, g):
        return remote(
            col_s.at[src, g], col_s.at[src, g], col_send.at[dst, g], col_recv.at[src, g], dst * n2 + b
        )

    def cm_copy(src, dst, g):
        return remote(
            col_m.at[src, g], col_m.at[src, g], cm_send.at[dst, g], cm_recv.at[src, g], dst * n2 + b
        )

    def cd_copy(src, dst):
        return remote(col_d.at[src], col_d.at[src], cd_send.at[dst], cd_recv.at[src], dst * n2 + b)

    gains[...] = gain_ref[...].astype(F32)

    rate = -jnp.exp(dlog_ref[...])
    below = lax.broadcasted_iota(jnp.int32, (SPAN, SPAN), 0)
    along = lax.broadcasted_iota(jnp.int32, (SPAN, SPAN), 1)
    causal = below >= along
    tri = causal.astype(F32)
    total = jnp.zeros((GROUPS * PER_GROUP, 1), F32)
    for c in range(spans):
        at = slice(c * SPAN, (c + 1) * SPAN)
        dt_rows = step_ref[:, at]
        dt = dt_rows.T
        cum = jnp.dot(tri, dt * rate, precision=lax.Precision.HIGHEST, preferred_element_type=F32)
        cum_tr = cum.T
        te = jnp.exp(cum[SPAN - 1 :, :] - cum) * dt
        ec = jnp.exp(cum)
        for g in range(GROUPS):
            hs = slice(g * PER_GROUP, (g + 1) * PER_GROUP)
            cum_g[g, at, :] = cum[:, hs]
            te_g[g, at, :] = te[:, hs]
            ec_g[g, at, :] = ec[:, hs]
        cum_t[:, at] = cum_tr
        dt_t[:, at] = dt_rows
        total = total + cum_tr[:, SPAN - 1 :]
    for g in range(GROUPS):
        hs = slice(g * PER_GROUP, (g + 1) * PER_GROUP)
        row_d[b, g, :, :] = jnp.broadcast_to(jnp.exp(total[hs, :]), (PER_GROUP, 128))
    each(0, n2, row_needed, lambda i: rd_copy(b, i).start())

    def end_decay(c, g):
        ends = cum_t[pl.ds(pl.multiple_of(g * PER_GROUP, 8), PER_GROUP), c * SPAN : (c + 1) * SPAN]
        return jnp.exp(jnp.broadcast_to(ends[:, SPAN - 1 :], (PER_GROUP, 128)))

    def states(g, _):
        for c in range(spans):
            at = slice(c * SPAN, (c + 1) * SPAN)
            te = te_g[g, at, :]
            wv = w_ref[at, lanes(g * STATE, STATE)]
            ed = end_decay(c, g)
            scaled = []
            for j in range(PER_GROUP):
                xv = x_ref[at, lanes(g * WIDE + j * HEAD_DIM, HEAD_DIM)].astype(F32)
                scaled.append((te[:, j : j + 1] * xv).astype(BF16))
            for j in range(0, PER_GROUP, 2):
                fresh = lax.dot_general(
                    wv, jnp.concatenate(scaled[j : j + 2], axis=1), TN, preferred_element_type=F32
                )
                for o in range(2):
                    js = slice((j + o) * HEAD_DIM, (j + o + 1) * HEAD_DIM)
                    part = fresh[:, o * HEAD_DIM : (o + 1) * HEAD_DIM]
                    if c:
                        part = ed[j + o : j + o + 1, :] * st0[c - 1, g, :, js] + part
                    if c < spans - 1:
                        st0[c, g, :, js] = part
                    else:
                        fin[g, :, js] = part
                        most = largest(part)
                        row_m[b, g, j + o : j + o + 1, :] = most
                        row_s[b, g, :, js] = coded(part, most)

        def go(i):
            rm_copy(b, i, g).start()
            row_copy(b, i, g).start()

        each(0, n2, row_needed, go)
        return _

    loads[0].wait()
    lax.fori_loop(0, GROUPS, states, 0)
    each(0, n2, lambda i: i > b, lambda i: key_own(i).start())

    def within(g, _):
        for c in range(spans):
            at = slice(c * SPAN, (c + 1) * SPAN)
            rv = r_ref[at, lanes(g * STATE, STATE)]
            wv = w_ref[at, lanes(g * STATE, STATE)]
            cross = lax.dot_general(rv, wv, NT, preferred_element_type=F32)
            hs = pl.ds(pl.multiple_of(g * PER_GROUP, 8), PER_GROUP)
            cum_rows = cum_t[hs, at]
            dt_rows = dt_t[hs, at]
            cum_cols = cum_g[g, at, :]
            for j in range(PER_GROUP):
                gap = cum_cols[:, j : j + 1] - cum_rows[j : j + 1, :]
                decay = jnp.exp(jnp.where(causal, jnp.minimum(gap, 0.0), -1e30))
                weights = (cross * decay * dt_rows[j : j + 1, :]).astype(BF16)
                xv = x_ref[at, lanes(g * WIDE + j * HEAD_DIM, HEAD_DIM)]
                y = jnp.dot(weights, xv, preferred_element_type=F32)
                loc[at, lanes(g * WIDE + j * HEAD_DIM, HEAD_DIM)] = (
                    y + skip_ref[g * PER_GROUP + j] * xv.astype(F32)
                )
        return _

    seen = lax.broadcasted_iota(jnp.int32, (rows, rows), 0) >= lax.broadcasted_iota(
        jnp.int32, (rows, rows), 1
    )

    def own(h, _):
        kv = k_ref[:, lanes(h * ATT_DIM, ATT_DIM)]
        vv = v_ref[:, lanes(h * ATT_DIM, ATT_DIM)]
        for r in range(REP):
            at = lanes((h * REP + r) * ATT_DIM, ATT_DIM)
            s = lax.dot_general(q_ref[:, at], kv, NT, preferred_element_type=F32) * scale
            s = jnp.where(seen, s, -1e30)
            top = jnp.max(s, axis=-1, keepdims=True)
            p = jnp.exp(s - top)
            mx[h * REP + r] = jnp.broadcast_to(top, (rows, 128))
            ls[h * REP + r] = jnp.broadcast_to(jnp.sum(p, axis=-1, keepdims=True), (rows, 128))
            acc[:, at] = jnp.dot(p.astype(BF16), vv, preferred_element_type=F32)
        return _

    each(0, n2, row_comes, lambda i: rd_copy(i, b).wait_recv())

    @pl.when(a < n1 - 1)
    def _row_total():
        col_d[a] = lax.fori_loop(
            0, n2, lambda i, d: d * row_d[i], jnp.ones((GROUPS, PER_GROUP, 128), F32)
        )

    each(0, n1, lambda i: i > a, lambda i: cd_copy(a, i).start())

    def row_phase(g, _):
        def come(i):
            rm_copy(i, b, g).wait_recv()
            row_copy(i, b, g).wait_recv()

        each(0, n2, row_comes, come)
        for j in range(PER_GROUP):
            js = slice(j * HEAD_DIM, (j + 1) * HEAD_DIM)

            def fold(i, t, j=j, js=js):
                new = decoded(row_s[i, g, :, js], row_m[i, g, j : j + 1, :])
                return row_d[i, g, j : j + 1, :] * t + new

            before = lax.fori_loop(0, b, fold, jnp.zeros((STATE, HEAD_DIM), F32))
            inc[g, :, js] = before

            @pl.when(a < n1 - 1)
            def _all(before=before, fold=fold, j=j, js=js):
                mine = row_d[b, g, j : j + 1, :] * before + fin[g, :, js]
                whole = lax.fori_loop(b + 1, n2, fold, mine)
                most = largest(whole)
                col_m[a, g, j : j + 1, :] = most
                col_s[a, g, :, js] = coded(whole, most)

        def go(i):
            cm_copy(a, i, g).start()
            col_copy(a, i, g).start()

        each(0, n1, lambda i: i > a, go)
        return _

    for later in loads[1:3]:
        later.wait()

    def hand_keys(src_a, _):
        got(0, src_a * n2 + b)
        each(0, n2, lambda i: i != b, lambda i: key_copy(src_a, i).start())
        return _

    lax.fori_loop(0, a, hand_keys, 0)

    def hand_values(src_b):
        got(1, a * n2 + src_b)
        each(0, n1, below_me, lambda i: value_copy(src_b, i).start())

    each(0, n2, row_comes, hand_values)

    def turn(g, _):
        within(g, 0)
        own(g, 0)

        @pl.when(a < n1 - 1)
        def _first():
            row_phase(g, 0)

        return _

    lax.fori_loop(0, GROUPS, turn, 0)

    def earlier(back, _):
        src = me - 1 - back

        @pl.when(src % n2 != b)
        def _key():
            got(0, src)

        @pl.when(src // n2 != a)
        def _value():
            got(1, src)

        def heads(h, _):
            kv = kbuf[src, :, lanes(h * ATT_DIM, ATT_DIM)]
            vv = vbuf[src, :, lanes(h * ATT_DIM, ATT_DIM)]
            for r in range(REP):
                at = lanes((h * REP + r) * ATT_DIM, ATT_DIM)
                s = lax.dot_general(q_ref[:, at], kv, NT, preferred_element_type=F32) * scale
                old = mx[h * REP + r]
                top = jnp.maximum(old, jnp.max(s, axis=-1, keepdims=True))
                factor = jnp.exp(old - top)
                p = jnp.exp(s - jnp.concatenate([top] * (rows // 128), axis=1))
                mx[h * REP + r] = top
                ls[h * REP + r] = ls[h * REP + r] * factor + jnp.sum(p, axis=-1, keepdims=True)
                acc[:, at] = acc[:, at] * factor + jnp.dot(
                    p.astype(BF16), vv, preferred_element_type=F32
                )
            return _

        lax.fori_loop(0, KV_HEADS, heads, 0)
        return _

    lax.fori_loop(0, me, earlier, 0)

    def close(h, _):
        at = lanes(h * ATT_DIM, ATT_DIM)
        att_ref[:, at] = (acc[:, at] / ls[h]).astype(BF16)
        return _

    lax.fori_loop(0, Q_HEADS, close, 0)

    @pl.when(a == n1 - 1)
    def _last():
        lax.fori_loop(0, GROUPS, row_phase, 0)

    loads[3].wait()
    each(0, n1, lambda i: i < a, lambda i: cd_copy(i, a).wait_recv())

    def finish(g, _):
        def come(i):
            cm_copy(i, a, g).wait_recv()
            col_copy(i, a, g).wait_recv()

        each(0, n1, lambda i: i < a, come)
        pre = lax.fori_loop(0, b, lambda i, d: d * row_d[i, g], jnp.ones((PER_GROUP, 128), F32))
        for j in range(PER_GROUP):
            js = slice(j * HEAD_DIM, (j + 1) * HEAD_DIM)

            def fold(i, t, j=j, js=js):
                new = decoded(col_s[i, g, :, js], col_m[i, g, j : j + 1, :])
                return col_d[i, g, j : j + 1, :] * t + new

            above = lax.fori_loop(0, a, fold, jnp.zeros((STATE, HEAD_DIM), F32))
            inc[g, :, js] = inc[g, :, js] + pre[j : j + 1, :] * above
        before = jnp.ones((PER_GROUP, 128), F32)
        for c in range(spans):
            at = slice(c * SPAN, (c + 1) * SPAN)
            rv = r_ref[at, lanes(g * STATE, STATE)]
            ec = ec_g[g, at, :]
            square = jnp.zeros((SPAN, HEAD_DIM), F32)
            for j in range(0, PER_GROUP, 2):
                starts = []
                for o in range(2):
                    js = slice((j + o) * HEAD_DIM, (j + o + 1) * HEAD_DIM)
                    start = inc[g, :, js]
                    if c:
                        start = before[j + o : j + o + 1, :] * start + st0[c - 1, g, :, js]
                    starts.append(start.astype(BF16))
                read = jnp.dot(rv, jnp.concatenate(starts, axis=1), preferred_element_type=F32)
                for o in range(2):
                    hs = lanes(g * WIDE + (j + o) * HEAD_DIM, HEAD_DIM)
                    mixed = (
                        loc[at, hs]
                        + read[:, o * HEAD_DIM : (o + 1) * HEAD_DIM] * ec[:, j + o : j + o + 1]
                    )
                    v = gate_ref[at, hs].astype(F32)
                    gated = mixed * (v / (1.0 + jnp.exp(-v)))
                    loc[at, hs] = gated
                    square = square + gated * gated
            mean = jnp.sum(square, axis=-1, keepdims=True) / WIDE
            inverse = lax.rsqrt(mean + 1e-05)
            gain = gains[pl.ds(pl.multiple_of(g * PER_GROUP, 8), PER_GROUP), :]
            for j in range(PER_GROUP):
                hs = lanes(g * WIDE + j * HEAD_DIM, HEAD_DIM)
                ssd_ref[at, hs] = (loc[at, hs] * inverse * gain[j : j + 1, :]).astype(BF16)
            before = before * end_decay(c, g)
        return _

    lax.fori_loop(0, GROUPS, finish, 0)

    each(0, n1, below_me, lambda i: key_down(i).wait_send())
    each(0, n2, row_needed, lambda i: value_own(i).wait_send())
    each(0, n1, below_me, lambda i: value_down(i).wait_send())
    each(0, n2, lambda i: i > b, lambda i: key_own(i).wait_send())

    def handed(src_a, _):
        each(0, n2, lambda i: i != b, lambda i: key_copy(src_a, i).wait_send())
        return _

    lax.fori_loop(0, a, handed, 0)
    each(
        0,
        n2,
        row_comes,
        lambda j: each(0, n1, below_me, lambda i: value_copy(j, i).wait_send()),
    )
    each(0, n2, row_needed, lambda i: rd_copy(b, i).wait_send())
    each(0, n1, lambda i: i > a, lambda i: cd_copy(a, i).wait_send())

    def sent(g, _):
        def row_left(i):
            rm_copy(b, i, g).wait_send()
            row_copy(b, i, g).wait_send()

        def col_left(i):
            cm_copy(a, i, g).wait_send()
            col_copy(a, i, g).wait_send()

        each(0, n2, row_needed, row_left)
        each(0, n1, lambda i: i > a, col_left)
        return _

    lax.fori_loop(0, GROUPS, sent, 0)


def local(
    n,
    ssd_input,
    gate_input,
    write_map,
    read_map,
    step_size,
    decay_log,
    skip_gain,
    norm_gain,
    query_rows,
    key_rows,
    value_rows,
):
    n2 = math.isqrt(n)
    while n % n2:
        n2 -= 1
    n1 = n // n2
    rows = ssd_input.shape[0]
    spans = rows // SPAN
    heads = GROUPS * PER_GROUP
    vmem = pl.BlockSpec(memory_space=pltpu.VMEM)
    hbm = pl.BlockSpec(memory_space=pl.ANY)
    smem = pl.BlockSpec(memory_space=pltpu.SMEM)
    dma = pltpu.SemaphoreType.DMA
    return pl.pallas_call(
        functools.partial(kernel, n, n1, n2),
        out_shape=(
            pltpu.VMEM(ssd_input.shape, BF16),
            pltpu.VMEM(query_rows.shape, BF16),
        ),
        in_specs=[hbm, hbm, vmem, hbm, vmem, vmem, smem, vmem, hbm, vmem, vmem],
        out_specs=(vmem, vmem),
        scratch_shapes=[
            pltpu.VMEM((n,) + key_rows.shape, BF16),
            pltpu.VMEM((n,) + value_rows.shape, BF16),
            pltpu.VMEM((n2, GROUPS, STATE, WIDE), BF16),
            pltpu.VMEM((n1, GROUPS, STATE, WIDE), BF16),
            pltpu.VMEM((n2, GROUPS, PER_GROUP, 128), F32),
            pltpu.VMEM((n1, GROUPS, PER_GROUP, 128), F32),
            pltpu.VMEM((n2, GROUPS, PER_GROUP, 128), F32),
            pltpu.VMEM((n1, GROUPS, PER_GROUP, 128), F32),
            pltpu.VMEM((GROUPS, STATE, WIDE), F32),
            pltpu.VMEM((heads, HEAD_DIM), F32),
            pltpu.VMEM(ssd_input.shape, BF16),
            pltpu.VMEM(gate_input.shape, BF16),
            pltpu.VMEM(read_map.shape, BF16),
            pltpu.VMEM(query_rows.shape, BF16),
            dma((4,)),
            pltpu.VMEM((GROUPS, rows, PER_GROUP), F32),
            pltpu.VMEM((GROUPS, rows, PER_GROUP), F32),
            pltpu.VMEM((GROUPS, rows, PER_GROUP), F32),
            pltpu.VMEM((heads, rows), F32),
            pltpu.VMEM((heads, rows), F32),
            pltpu.VMEM((spans - 1, GROUPS, STATE, WIDE), F32),
            pltpu.VMEM((GROUPS, STATE, WIDE), F32),
            pltpu.VMEM(ssd_input.shape, F32),
            pltpu.VMEM(query_rows.shape, F32),
            pltpu.VMEM((Q_HEADS, rows, 128), F32),
            pltpu.VMEM((Q_HEADS, rows, 128), F32),
            dma((n1, n2)),
            dma((n1,)),
            dma((n2,)),
            dma((n2, n1)),
            dma((2, n)),
            dma((n2, GROUPS)),
            dma((n2, GROUPS)),
            dma((n1, GROUPS)),
            dma((n1, GROUPS)),
            dma((n2, GROUPS)),
            dma((n2, GROUPS)),
            dma((n1, GROUPS)),
            dma((n1, GROUPS)),
            dma((n2,)),
            dma((n2,)),
            dma((n1,)),
            dma((n1,)),
        ],
        compiler_params=pltpu.CompilerParams(
            collective_id=0, has_side_effects=True, vmem_limit_bytes=58 * 2**20
        ),
        cost_estimate=pl.CostEstimate(
            flops=4 * 10**9, bytes_accessed=12 * 2**20, transcendentals=6 * 10**6
        ),
        name="hybrid_cores",
    )(
        ssd_input,
        gate_input,
        write_map,
        read_map,
        step_size.T,
        decay_log.reshape(1, -1),
        skip_gain,
        norm_gain.reshape(-1, HEAD_DIM),
        query_rows,
        key_rows,
        value_rows,
    )


def solution(mesh):
    split = P(("dp", "seq"), None)
    in_specs = (split, split, split, split, split, P(), P(), P(), split, split, split)
    body = functools.partial(local, mesh.shape["seq"])
    return jax.shard_map(
        body, mesh=mesh, in_specs=in_specs, out_specs=(split, split), check_vma=False
    )
```

```python
import functools
import math

import jax
import jax.numpy as jnp
from jax import lax
from jax.experimental import pallas as pl
from jax.experimental.pallas import tpu as pltpu
from jax.sharding import PartitionSpec as P

HEAD_DIM = 128
STATE = 128
GROUPS = 4
PER_GROUP = 8
SPAN = 128
Q_HEADS = 16
KV_HEADS = 4
REP = Q_HEADS // KV_HEADS
ATT_DIM = 128
WIDE = PER_GROUP * HEAD_DIM
F32 = jnp.float32
BF16 = jnp.bfloat16
LOWEST = 125.0 * math.log(2.0)
REACH = 250.0 * math.log(2.0)
NT = (((1,), (1,)), ((), ()))
TN = (((0,), (0,)), ((), ()))


def lanes(start, size):
    return pl.ds(pl.multiple_of(start, 128), size)


def coded(value, most):
    root = jnp.sqrt(jnp.abs(value) * (1.0 / most))
    size = jnp.exp(root * REACH - LOWEST)
    return jnp.where(value < 0.0, -size, size).astype(BF16)


def decoded(code, most):
    wide = code.astype(F32)
    root = jnp.maximum(jnp.log(jnp.abs(wide)) + LOWEST, 0.0) * (1.0 / REACH)
    size = root * root * most
    return jnp.where(wide < 0.0, -size, size)


def largest(value):
    column = jnp.max(jnp.abs(value), axis=0, keepdims=True)
    most = jnp.max(column, axis=1, keepdims=True)
    return jnp.broadcast_to(jnp.maximum(most, 1e-30), (1, 128))


def remote(src, dst, send, recv, target):
    return pltpu.make_async_remote_copy(
        src_ref=src,
        dst_ref=dst,
        send_sem=send,
        recv_sem=recv,
        device_id={"seq": target},
        device_id_type=pl.DeviceIdType.MESH,
    )


def kernel(
    n,
    n1,
    n2,
    x_hbm,
    gate_hbm,
    w_ref,
    r_hbm,
    step_ref,
    dlog_ref,
    skip_ref,
    gain_ref,
    q_hbm,
    k_ref,
    v_ref,
    ssd_ref,
    att_ref,
    kbuf,
    vbuf,
    row_s,
    col_s,
    row_d,
    col_d,
    row_m,
    col_m,
    fin,
    gains,
    x_ref,
    gate_ref,
    r_ref,
    q_ref,
    load,
    cum_g,
    te_g,
    ec_g,
    cum_t,
    dt_t,
    st0,
    inc,
    loc,
    acc,
    mx,
    ls,
    key_row,
    key_col,
    val_row,
    val_col,
    kv_recv,
    row_send,
    row_recv,
    col_send,
    col_recv,
    rm_send,
    rm_recv,
    cm_send,
    cm_recv,
    rd_send,
    rd_recv,
    cd_send,
    cd_recv,
):
    me = lax.axis_index("seq")
    a = me // n2
    b = me % n2
    rows = x_hbm.shape[0]
    spans = rows // SPAN
    scale = ATT_DIM**-0.5

    loads = [
        pltpu.make_async_copy(src, dst, load.at[i])
        for i, (src, dst) in enumerate(
            ((x_hbm, x_ref), (r_hbm, r_ref), (q_hbm, q_ref), (gate_hbm, gate_ref))
        )
    ]
    loads[0].start()

    barrier = pltpu.get_barrier_semaphore()

    def greet(i, _):
        pl.semaphore_signal(
            barrier,
            inc=1,
            device_id={"seq": lax.rem(me + i, n)},
            device_id_type=pl.DeviceIdType.MESH,
        )
        return _

    lax.fori_loop(1, n, greet, 0)
    pl.semaphore_wait(barrier, n - 1)

    def each(lo, hi, needed, act):
        def body(i, _):
            @pl.when(needed(i))
            def _go():
                act(i)

            return _

        lax.fori_loop(lo, hi, body, 0)

    def key_copy(src_a, dst_b):
        src = src_a * n2 + b
        return remote(
            kbuf.at[src], kbuf.at[src], key_row.at[src_a, dst_b], kv_recv.at[0, src], a * n2 + dst_b
        )

    def key_down(dst_a):
        return remote(k_ref, kbuf.at[me], key_col.at[dst_a], kv_recv.at[0, me], dst_a * n2 + b)

    def key_own(dst_b):
        return remote(k_ref, kbuf.at[me], key_row.at[a, dst_b], kv_recv.at[0, me], a * n2 + dst_b)

    def value_copy(src_b, dst_a):
        src = a * n2 + src_b
        return remote(
            vbuf.at[src], vbuf.at[src], val_col.at[src_b, dst_a], kv_recv.at[1, src], dst_a * n2 + b
        )

    def value_down(dst_a):
        return remote(v_ref, vbuf.at[me], val_col.at[b, dst_a], kv_recv.at[1, me], dst_a * n2 + b)

    def value_own(dst_b):
        return remote(v_ref, vbuf.at[me], val_row.at[dst_b], kv_recv.at[1, me], a * n2 + dst_b)

    def got(which, src):
        return remote(k_ref, kbuf.at[src], key_col.at[0], kv_recv.at[which, src], src).wait_recv()

    def below_me(i):
        return i > a

    def row_needed(i):
        return (i != b) & ((i > b) | (a < n1 - 1))

    def row_comes(i):
        return (i != b) & ((i < b) | (a < n1 - 1))

    each(0, n1, below_me, lambda i: key_down(i).start())
    each(0, n2, row_needed, lambda i: value_own(i).start())
    each(0, n1, below_me, lambda i: value_down(i).start())
    for later in loads[1:]:
        later.start()

    def row_copy(src, dst, g):
        return remote(
            row_s.at[src, g], row_s.at[src, g], row_send.at[dst, g], row_recv.at[src, g], a * n2 + dst
        )

    def rm_copy(src, dst, g):
        return remote(
            row_m.at[src, g], row_m.at[src, g], rm_send.at[dst, g], rm_recv.at[src, g], a * n2 + dst
        )

    def rd_copy(src, dst):
        return remote(row_d.at[src], row_d.at[src], rd_send.at[dst], rd_recv.at[src], a * n2 + dst)

    def col_copy(src, dst, g):
        return remote(
            col_s.at[src, g], col_s.at[src, g], col_send.at[dst, g], col_recv.at[src, g], dst * n2 + b
        )

    def cm_copy(src, dst, g):
        return remote(
            col_m.at[src, g], col_m.at[src, g], cm_send.at[dst, g], cm_recv.at[src, g], dst * n2 + b
        )

    def cd_copy(src, dst):
        return remote(col_d.at[src], col_d.at[src], cd_send.at[dst], cd_recv.at[src], dst * n2 + b)

    gains[...] = gain_ref[...].astype(F32)

    rate = -jnp.exp(dlog_ref[...])
    below = lax.broadcasted_iota(jnp.int32, (SPAN, SPAN), 0)
    along = lax.broadcasted_iota(jnp.int32, (SPAN, SPAN), 1)
    causal = below >= along
    tri = causal.astype(F32)
    total = jnp.zeros((GROUPS * PER_GROUP, 1), F32)
    for c in range(spans):
        at = slice(c * SPAN, (c + 1) * SPAN)
        dt_rows = step_ref[:, at]
        dt = dt_rows.T
        cum = jnp.dot(tri, dt * rate, precision=lax.Precision.HIGHEST, preferred_element_type=F32)
        cum_tr = cum.T
        te = jnp.exp(cum[SPAN - 1 :, :] - cum) * dt
        ec = jnp.exp(cum)
        for g in range(GROUPS):
            hs = slice(g * PER_GROUP, (g + 1) * PER_GROUP)
            cum_g[g, at, :] = cum[:, hs]
            te_g[g, at, :] = te[:, hs]
            ec_g[g, at, :] = ec[:, hs]
        cum_t[:, at] = cum_tr
        dt_t[:, at] = dt_rows
        total = total + cum_tr[:, SPAN - 1 :]
    for g in range(GROUPS):
        hs = slice(g * PER_GROUP, (g + 1) * PER_GROUP)
        row_d[b, g, :, :] = jnp.broadcast_to(jnp.exp(total[hs, :]), (PER_GROUP, 128))
    each(0, n2, row_needed, lambda i: rd_copy(b, i).start())

    def end_decay(c, g):
        ends = cum_t[pl.ds(pl.multiple_of(g * PER_GROUP, 8), PER_GROUP), c * SPAN : (c + 1) * SPAN]
        return jnp.exp(jnp.broadcast_to(ends[:, SPAN - 1 :], (PER_GROUP, 128)))

    def hand_keys(src_a, _):
        got(0, src_a * n2 + b)
        each(0, n2, lambda i: i != b, lambda i: key_copy(src_a, i).start())
        return _

    def states(g, _):
        for c in range(spans):
            at = slice(c * SPAN, (c + 1) * SPAN)
            te = te_g[g, at, :]
            wv = w_ref[at, lanes(g * STATE, STATE)]
            ed = end_decay(c, g)
            scaled = []
            for j in range(PER_GROUP):
                xv = x_ref[at, lanes(g * WIDE + j * HEAD_DIM, HEAD_DIM)].astype(F32)
                scaled.append((te[:, j : j + 1] * xv).astype(BF16))
            for j in range(0, PER_GROUP, 2):
                fresh = lax.dot_general(
                    wv, jnp.concatenate(scaled[j : j + 2], axis=1), TN, preferred_element_type=F32
                )
                for o in range(2):
                    js = slice((j + o) * HEAD_DIM, (j + o + 1) * HEAD_DIM)
                    part = fresh[:, o * HEAD_DIM : (o + 1) * HEAD_DIM]
                    if c:
                        part = ed[j + o : j + o + 1, :] * st0[c - 1, g, :, js] + part
                    if c < spans - 1:
                        st0[c, g, :, js] = part
                    else:
                        fin[g, :, js] = part
                        most = largest(part)
                        row_m[b, g, j + o : j + o + 1, :] = most
                        row_s[b, g, :, js] = coded(part, most)

        def go(i):
            rm_copy(b, i, g).start()
            row_copy(b, i, g).start()

        @pl.when(g == 1)
        def _keys():
            lax.fori_loop(0, a, hand_keys, 0)

        each(0, n2, row_needed, go)
        return _

    loads[0].wait()
    lax.fori_loop(0, GROUPS, states, 0)
    each(0, n2, lambda i: i > b, lambda i: key_own(i).start())

    def within(g, _):
        for c in range(spans):
            at = slice(c * SPAN, (c + 1) * SPAN)
            rv = r_ref[at, lanes(g * STATE, STATE)]
            wv = w_ref[at, lanes(g * STATE, STATE)]
            cross = lax.dot_general(rv, wv, NT, preferred_element_type=F32)
            hs = pl.ds(pl.multiple_of(g * PER_GROUP, 8), PER_GROUP)
            cum_rows = cum_t[hs, at]
            dt_rows = dt_t[hs, at]
            cum_cols = cum_g[g, at, :]
            for j in range(PER_GROUP):
                gap = cum_cols[:, j : j + 1] - cum_rows[j : j + 1, :]
                decay = jnp.exp(jnp.where(causal, jnp.minimum(gap, 0.0), -1e30))
                weights = (cross * decay * dt_rows[j : j + 1, :]).astype(BF16)
                xv = x_ref[at, lanes(g * WIDE + j * HEAD_DIM, HEAD_DIM)]
                y = jnp.dot(weights, xv, preferred_element_type=F32)
                loc[at, lanes(g * WIDE + j * HEAD_DIM, HEAD_DIM)] = (
                    y + skip_ref[g * PER_GROUP + j] * xv.astype(F32)
                )
        return _

    seen = lax.broadcasted_iota(jnp.int32, (rows, rows), 0) >= lax.broadcasted_iota(
        jnp.int32, (rows, rows), 1
    )

    def own(h, _):
        kv = k_ref[:, lanes(h * ATT_DIM, ATT_DIM)]
        vv = v_ref[:, lanes(h * ATT_DIM, ATT_DIM)]
        for r in range(REP):
            at = lanes((h * REP + r) * ATT_DIM, ATT_DIM)
            s = lax.dot_general(q_ref[:, at], kv, NT, preferred_element_type=F32) * scale
            s = jnp.where(seen, s, -1e30)
            top = jnp.max(s, axis=-1, keepdims=True)
            p = jnp.exp(s - top)
            mx[h * REP + r] = jnp.broadcast_to(top, (rows, 128))
            ls[h * REP + r] = jnp.broadcast_to(jnp.sum(p, axis=-1, keepdims=True), (rows, 128))
            acc[:, at] = jnp.dot(p.astype(BF16), vv, preferred_element_type=F32)
        return _

    each(0, n2, row_comes, lambda i: rd_copy(i, b).wait_recv())

    @pl.when(a < n1 - 1)
    def _row_total():
        col_d[a] = lax.fori_loop(
            0, n2, lambda i, d: d * row_d[i], jnp.ones((GROUPS, PER_GROUP, 128), F32)
        )

    each(0, n1, lambda i: i > a, lambda i: cd_copy(a, i).start())

    def row_phase(g, _):
        def come(i):
            rm_copy(i, b, g).wait_recv()
            row_copy(i, b, g).wait_recv()

        each(0, n2, row_comes, come)
        for j in range(PER_GROUP):
            js = slice(j * HEAD_DIM, (j + 1) * HEAD_DIM)

            def fold(i, t, j=j, js=js):
                new = decoded(row_s[i, g, :, js], row_m[i, g, j : j + 1, :])
                return row_d[i, g, j : j + 1, :] * t + new

            before = lax.fori_loop(0, b, fold, jnp.zeros((STATE, HEAD_DIM), F32))
            inc[g, :, js] = before

            @pl.when(a < n1 - 1)
            def _all(before=before, fold=fold, j=j, js=js):
                mine = row_d[b, g, j : j + 1, :] * before + fin[g, :, js]
                whole = lax.fori_loop(b + 1, n2, fold, mine)
                most = largest(whole)
                col_m[a, g, j : j + 1, :] = most
                col_s[a, g, :, js] = coded(whole, most)

        def go(i):
            cm_copy(a, i, g).start()
            col_copy(a, i, g).start()

        each(0, n1, lambda i: i > a, go)
        return _

    for later in loads[1:3]:
        later.wait()

    def hand_values(src_b):
        got(1, a * n2 + src_b)
        each(0, n1, below_me, lambda i: value_copy(src_b, i).start())

    each(0, n2, row_comes, hand_values)

    def turn(g, _):
        within(g, 0)
        own(g, 0)

        @pl.when(a < n1 - 1)
        def _first():
            row_phase(g, 0)

        return _

    lax.fori_loop(0, GROUPS, turn, 0)

    def earlier(back, _):
        src = me - 1 - back

        @pl.when(src % n2 != b)
        def _key():
            got(0, src)

        @pl.when(src // n2 != a)
        def _value():
            got(1, src)

        def heads(h, _):
            kv = kbuf[src, :, lanes(h * ATT_DIM, ATT_DIM)]
            vv = vbuf[src, :, lanes(h * ATT_DIM, ATT_DIM)]
            for r in range(REP):
                at = lanes((h * REP + r) * ATT_DIM, ATT_DIM)
                s = lax.dot_general(q_ref[:, at], kv, NT, preferred_element_type=F32) * scale
                old = mx[h * REP + r]
                top = jnp.maximum(old, jnp.max(s, axis=-1, keepdims=True))
                factor = jnp.exp(old - top)
                p = jnp.exp(s - jnp.concatenate([top] * (rows // 128), axis=1))
                mx[h * REP + r] = top
                ls[h * REP + r] = ls[h * REP + r] * factor + jnp.sum(p, axis=-1, keepdims=True)
                acc[:, at] = acc[:, at] * factor + jnp.dot(
                    p.astype(BF16), vv, preferred_element_type=F32
                )
            return _

        lax.fori_loop(0, KV_HEADS, heads, 0)
        return _

    lax.fori_loop(0, me, earlier, 0)

    def close(h, _):
        at = lanes(h * ATT_DIM, ATT_DIM)
        att_ref[:, at] = (acc[:, at] / ls[h]).astype(BF16)
        return _

    lax.fori_loop(0, Q_HEADS, close, 0)

    @pl.when(a == n1 - 1)
    def _last():
        lax.fori_loop(0, GROUPS, row_phase, 0)

    loads[3].wait()
    each(0, n1, lambda i: i < a, lambda i: cd_copy(i, a).wait_recv())

    def finish(g, _):
        def come(i):
            cm_copy(i, a, g).wait_recv()
            col_copy(i, a, g).wait_recv()

        each(0, n1, lambda i: i < a, come)
        pre = lax.fori_loop(0, b, lambda i, d: d * row_d[i, g], jnp.ones((PER_GROUP, 128), F32))
        for j in range(PER_GROUP):
            js = slice(j * HEAD_DIM, (j + 1) * HEAD_DIM)

            def fold(i, t, j=j, js=js):
                new = decoded(col_s[i, g, :, js], col_m[i, g, j : j + 1, :])
                return col_d[i, g, j : j + 1, :] * t + new

            above = lax.fori_loop(0, a, fold, jnp.zeros((STATE, HEAD_DIM), F32))
            inc[g, :, js] = inc[g, :, js] + pre[j : j + 1, :] * above
        before = jnp.ones((PER_GROUP, 128), F32)
        for c in range(spans):
            at = slice(c * SPAN, (c + 1) * SPAN)
            rv = r_ref[at, lanes(g * STATE, STATE)]
            ec = ec_g[g, at, :]
            square = jnp.zeros((SPAN, HEAD_DIM), F32)
            for j in range(0, PER_GROUP, 2):
                starts = []
                for o in range(2):
                    js = slice((j + o) * HEAD_DIM, (j + o + 1) * HEAD_DIM)
                    start = inc[g, :, js]
                    if c:
                        start = before[j + o : j + o + 1, :] * start + st0[c - 1, g, :, js]
                    starts.append(start.astype(BF16))
                read = jnp.dot(rv, jnp.concatenate(starts, axis=1), preferred_element_type=F32)
                for o in range(2):
                    hs = lanes(g * WIDE + (j + o) * HEAD_DIM, HEAD_DIM)
                    mixed = (
                        loc[at, hs]
                        + read[:, o * HEAD_DIM : (o + 1) * HEAD_DIM] * ec[:, j + o : j + o + 1]
                    )
                    v = gate_ref[at, hs].astype(F32)
                    gated = mixed * (v / (1.0 + jnp.exp(-v)))
                    loc[at, hs] = gated
                    square = square + gated * gated
            mean = jnp.sum(square, axis=-1, keepdims=True) / WIDE
            inverse = lax.rsqrt(mean + 1e-05)
            gain = gains[pl.ds(pl.multiple_of(g * PER_GROUP, 8), PER_GROUP), :]
            for j in range(PER_GROUP):
                hs = lanes(g * WIDE + j * HEAD_DIM, HEAD_DIM)
                ssd_ref[at, hs] = (loc[at, hs] * inverse * gain[j : j + 1, :]).astype(BF16)
            before = before * end_decay(c, g)
        return _

    lax.fori_loop(0, GROUPS, finish, 0)

    each(0, n1, below_me, lambda i: key_down(i).wait_send())
    each(0, n2, row_needed, lambda i: value_own(i).wait_send())
    each(0, n1, below_me, lambda i: value_down(i).wait_send())
    each(0, n2, lambda i: i > b, lambda i: key_own(i).wait_send())

    def handed(src_a, _):
        each(0, n2, lambda i: i != b, lambda i: key_copy(src_a, i).wait_send())
        return _

    lax.fori_loop(0, a, handed, 0)
    each(
        0,
        n2,
        row_comes,
        lambda j: each(0, n1, below_me, lambda i: value_copy(j, i).wait_send()),
    )
    each(0, n2, row_needed, lambda i: rd_copy(b, i).wait_send())
    each(0, n1, lambda i: i > a, lambda i: cd_copy(a, i).wait_send())

    def sent(g, _):
        def row_left(i):
            rm_copy(b, i, g).wait_send()
            row_copy(b, i, g).wait_send()

        def col_left(i):
            cm_copy(a, i, g).wait_send()
            col_copy(a, i, g).wait_send()

        each(0, n2, row_needed, row_left)
        each(0, n1, lambda i: i > a, col_left)
        return _

    lax.fori_loop(0, GROUPS, sent, 0)


def local(
    n,
    ssd_input,
    gate_input,
    write_map,
    read_map,
    step_size,
    decay_log,
    skip_gain,
    norm_gain,
    query_rows,
    key_rows,
    value_rows,
):
    n2 = math.isqrt(n)
    while n % n2:
        n2 -= 1
    n1 = n // n2
    rows = ssd_input.shape[0]
    spans = rows // SPAN
    heads = GROUPS * PER_GROUP
    vmem = pl.BlockSpec(memory_space=pltpu.VMEM)
    hbm = pl.BlockSpec(memory_space=pl.ANY)
    smem = pl.BlockSpec(memory_space=pltpu.SMEM)
    dma = pltpu.SemaphoreType.DMA
    return pl.pallas_call(
        functools.partial(kernel, n, n1, n2),
        out_shape=(
            pltpu.VMEM(ssd_input.shape, BF16),
            pltpu.VMEM(query_rows.shape, BF16),
        ),
        in_specs=[hbm, hbm, vmem, hbm, vmem, vmem, smem, vmem, hbm, vmem, vmem],
        out_specs=(vmem, vmem),
        scratch_shapes=[
            pltpu.VMEM((n,) + key_rows.shape, BF16),
            pltpu.VMEM((n,) + value_rows.shape, BF16),
            pltpu.VMEM((n2, GROUPS, STATE, WIDE), BF16),
            pltpu.VMEM((n1, GROUPS, STATE, WIDE), BF16),
            pltpu.VMEM((n2, GROUPS, PER_GROUP, 128), F32),
            pltpu.VMEM((n1, GROUPS, PER_GROUP, 128), F32),
            pltpu.VMEM((n2, GROUPS, PER_GROUP, 128), F32),
            pltpu.VMEM((n1, GROUPS, PER_GROUP, 128), F32),
            pltpu.VMEM((GROUPS, STATE, WIDE), F32),
            pltpu.VMEM((heads, HEAD_DIM), F32),
            pltpu.VMEM(ssd_input.shape, BF16),
            pltpu.VMEM(gate_input.shape, BF16),
            pltpu.VMEM(read_map.shape, BF16),
            pltpu.VMEM(query_rows.shape, BF16),
            dma((4,)),
            pltpu.VMEM((GROUPS, rows, PER_GROUP), F32),
            pltpu.VMEM((GROUPS, rows, PER_GROUP), F32),
            pltpu.VMEM((GROUPS, rows, PER_GROUP), F32),
            pltpu.VMEM((heads, rows), F32),
            pltpu.VMEM((heads, rows), F32),
            pltpu.VMEM((spans - 1, GROUPS, STATE, WIDE), F32),
            pltpu.VMEM((GROUPS, STATE, WIDE), F32),
            pltpu.VMEM(ssd_input.shape, F32),
            pltpu.VMEM(query_rows.shape, F32),
            pltpu.VMEM((Q_HEADS, rows, 128), F32),
            pltpu.VMEM((Q_HEADS, rows, 128), F32),
            dma((n1, n2)),
            dma((n1,)),
            dma((n2,)),
            dma((n2, n1)),
            dma((2, n)),
            dma((n2, GROUPS)),
            dma((n2, GROUPS)),
            dma((n1, GROUPS)),
            dma((n1, GROUPS)),
            dma((n2, GROUPS)),
            dma((n2, GROUPS)),
            dma((n1, GROUPS)),
            dma((n1, GROUPS)),
            dma((n2,)),
            dma((n2,)),
            dma((n1,)),
            dma((n1,)),
        ],
        compiler_params=pltpu.CompilerParams(
            collective_id=0, has_side_effects=True, vmem_limit_bytes=58 * 2**20
        ),
        cost_estimate=pl.CostEstimate(
            flops=4 * 10**9, bytes_accessed=12 * 2**20, transcendentals=6 * 10**6
        ),
        name="hybrid_cores",
    )(
        ssd_input,
        gate_input,
        write_map,
        read_map,
        step_size.T,
        decay_log.reshape(1, -1),
        skip_gain,
        norm_gain.reshape(-1, HEAD_DIM),
        query_rows,
        key_rows,
        value_rows,
    )


def solution(mesh):
    split = P(("dp", "seq"), None)
    in_specs = (split, split, split, split, split, P(), P(), P(), split, split, split)
    body = functools.partial(local, mesh.shape["seq"])
    return jax.shard_map(
        body, mesh=mesh, in_specs=in_specs, out_specs=(split, split), check_vma=False
    )
```
